128 devices in a mesh: island: 4 (over x_lo, core), fsdp: 32 (over x_hi, z, y).
Axes of the slice: x: 4 (x_hi: 2, x_lo: 2; x = x_hi * 2 + x_lo), y: 4, z: 4, core: 2. Of those that a mesh axis runs over, the one named last changes fastest.
Arguments:
- tokens: bfloat16 [4, 512, 4096], P('island', 'fsdp'), may hold values from -6 to 6
- w_gate: bfloat16 [4, 4096, 28672], P('island', None, 'fsdp'), may hold values from -6 to 6
- w_up: bfloat16 [4, 4096, 28672], P('island', None, 'fsdp'), may hold values from -6 to 6
- d_hidden: bfloat16 [4, 512, 28672], P('island', None, 'fsdp'), may hold values from -6 to 6
- outer_rows: float32 [2, 128, 28672], P(None, None, 'fsdp'), may hold values from -6 to 6
- outer_momentum: float32 [2, 128, 28672], P(None, None, 'fsdp'), may hold values from -4 to 4
- adam_first: float32 [4, 2, 128, 28672], P('island', None, None, 'fsdp'), may hold values from -3 to 3
- adam_second: float32 [4, 2, 128, 28672], P('island', None, None, 'fsdp'), may hold values from 0.04 to 1
- fragment_rows: int32 [128], replicated, may hold values from 0 to 4095, as said below
Outputs:
- d_tokens: bfloat16 [4, 512, 4096], P('island', 'fsdp')
- fragment_weights: bfloat16 [4, 2, 128, 28672], P('island', None, None, 'fsdp')
- outer_new: float32 [2, 128, 28672], P(None, None, 'fsdp')
- momentum_new: float32 [2, 128, 28672], P(None, None, 'fsdp')
- first_new: float32 [4, 2, 128, 28672], P('island', None, None, 'fsdp')
- second_new: float32 [4, 2, 128, 28672], P('island', None, None, 'fsdp')
The draws below stay inside these ranges and needn't reach their ends.
Inputs may be any that keep to these rules, and one draw needn't show every extreme that they name: `fragment_rows`: distinct row numbers.
All inputs are finite; a program needn't handle non-finite values.
Results may differ from the reference program's by a relative error of at most 0.005.
Values may be sent and summed in bfloat16 or wider, within the bound.
A program may use at most 128 MiB of HBM per device.

```python
import math
import jax
import jax.numpy as jnp
from jax import lax

D = 4096
FF = 28672
FRAG = 128
TOKENS = 512
N_ISLAND = 4


def draw_fragment_rows(key, part):
    key = jax.random.fold_in(key, 11)
    return jax.random.permutation(key, D)[:FRAG].astype(jnp.int32)


def shard_levels(rng, extent, pieces, smallest, high):
    loudness = 1.0
    for dim, parts in pieces:
        draws = jax.random.uniform(jax.random.fold_in(jax.random.fold_in(rng, 6), dim), (parts,), jnp.float32, smallest / len(pieces), high / len(pieces))
        loudness = loudness * jnp.repeat(jnp.exp(draws), extent[dim] // parts).reshape((-1,) + (1,) * (len(extent) - 1 - dim))
    return loudness


def normal_values(stream_key, dims, width, most, cuts=(), dtype=jnp.bfloat16):
    level = shard_levels(stream_key, dims, cuts, -0.22, 0.18) if cuts else 1.0
    values = jax.random.normal(stream_key, dims, jnp.float32) * width * level
    return jnp.minimum(jnp.maximum(values, -most), most).astype(dtype)


def setup_inputs(seed: int = 0) -> dict:
    streams_of = jax.random.split(jax.random.key(seed), 10)
    tokens = normal_values(streams_of[0], (N_ISLAND, TOKENS, D), 1.0, 6.0, ((0, 4), (1, 32)))
    w_gate = normal_values(streams_of[1], (N_ISLAND, D, FF), 1.0, 6.0, ((0, 4), (2, 32)))
    w_up = normal_values(streams_of[2], (N_ISLAND, D, FF), 1.0, 6.0, ((0, 4), (2, 32)))
    d_hidden = normal_values(streams_of[3], (N_ISLAND, TOKENS, FF), 1.0, 6.0, ((0, 4), (2, 32)))
    outer_rows = normal_values(streams_of[4], (2, FRAG, FF), 1.0, 6.0, ((2, 32),), jnp.float32)
    outer_momentum = normal_values(streams_of[5], (2, FRAG, FF), 0.5, 4.0, ((2, 32),), jnp.float32)
    adam_first = normal_values(streams_of[6], (N_ISLAND, 2, FRAG, FF), 0.3, 3.0, ((0, 4), (3, 32)), jnp.float32)
    adam_second = jnp.clip(jnp.exp(math.log(1.0) - 3.218876 * jax.random.uniform(streams_of[7], (N_ISLAND, 2, FRAG, FF), jnp.float32) ** shard_levels(streams_of[7], (N_ISLAND, 2, FRAG, FF), ((0, 4), (3, 32)), -0.2, 0.2)), 0.04, 1.0)
    fragment_rows = draw_fragment_rows(jax.random.fold_in(streams_of[9], 71), 0)
    return {"tokens": tokens, "w_gate": w_gate, "w_up": w_up, "d_hidden": d_hidden, "outer_rows": outer_rows, "outer_momentum": outer_momentum, "adam_first": adam_first, "adam_second": adam_second, "fragment_rows": fragment_rows}


def silu_parts(gate_pre):
    sigmoid_val = jax.nn.sigmoid(gate_pre)
    return (gate_pre * sigmoid_val, sigmoid_val * (1.0 + gate_pre * (1.0 - sigmoid_val)))

def reference(tokens, w_gate, w_up, d_hidden, outer_rows, outer_momentum, adam_first, adam_second, fragment_rows):
    factor = float(D) ** (-0.5)
    input_list = []
    pseudo_list = []
    gradient_list = []
    for island in range(N_ISLAND):
        activ = tokens[island]
        gate_weights = w_gate[island]
        up_weights = w_up[island]
        gate_pre = jnp.dot(activ, gate_weights, preferred_element_type=jnp.float32) * factor
        up_pre = jnp.dot(activ, up_weights, preferred_element_type=jnp.float32) * factor
        silu_value, silu_slope = silu_parts(gate_pre)
        upstream = d_hidden[island].astype(jnp.float32)
        d_gate = (upstream * up_pre * silu_slope).astype(jnp.bfloat16)
        d_up = (upstream * silu_value).astype(jnp.bfloat16)
        contract = (((1,), (1,)), ((), ()))
        input_grad = lax.dot_general(d_gate, gate_weights, contract, preferred_element_type=jnp.float32)
        input_grad = input_grad + lax.dot_general(d_up, up_weights, contract, preferred_element_type=jnp.float32)
        input_list.append((input_grad * factor).astype(jnp.bfloat16))
        picked = jnp.take(activ, fragment_rows, axis=1)
        over_tokens = (((0,), (0,)), ((), ()))
        gradient = jnp.stack([lax.dot_general(picked, d_gate, over_tokens, preferred_element_type=jnp.float32), lax.dot_general(picked, d_up, over_tokens, preferred_element_type=jnp.float32)]) * factor
        gradient_list.append(gradient)
        island_rows = jnp.stack([jnp.take(gate_weights, fragment_rows, axis=0), jnp.take(up_weights, fragment_rows, axis=0)]).astype(jnp.float32)
        pseudo_list.append(outer_rows - island_rows)
    total = pseudo_list[0]
    for island in range(1, N_ISLAND):
        total = total + pseudo_list[island]
    mean_delta = total / float(N_ISLAND)
    momentum_new = 0.9 * outer_momentum + mean_delta
    outer_new = outer_rows - 0.7 * (mean_delta + 0.9 * momentum_new)
    first_new = 0.9 * adam_first + 0.1 * jnp.stack(gradient_list)
    second_new = 0.95 * adam_second + 0.05 * jnp.stack(gradient_list) ** 2
    weights_new = outer_new[None] * (1.0 - 0.02 * 0.1) - 0.02 * first_new / (jnp.sqrt(second_new) + 1e-08)
    return (jnp.stack(input_list), weights_new.astype(jnp.bfloat16), outer_new, momentum_new, first_new, second_new)
```

```python
import functools

import jax
import jax.numpy as jnp
from jax import lax
from jax.experimental import pallas as pl
from jax.experimental.pallas import tpu as pltpu
from jax.sharding import PartitionSpec as P

MESH = pl.DeviceIdType.MESH
BF = jnp.bfloat16
F32 = jnp.float32

D = 4096
HID = 896
W2 = 2 * HID
TOK = 512
OWN = 16
FRAG = 128
NP = 4
NC = 2 * NP
DC = D // NC
HC = DC // 2
PC = 2 * DC
FACTOR = float(D) ** (-0.5)

AG = 9
RS = 9


def step_kernel(
    tok_hbm, wg_hbm, wu_hbm, dh_hbm, row_ref, col_ref,
    dtok_hbm, grad_hbm, rsum_hbm,
    wts, toks, acc, dcat, dhid, part, oh, oht, pick, rowp, rows_all, gradv, rsumv, dtokv,
    sb1, rb1, sb2, rb2, quart, last, sbx, rbx,
    w_sem, l_sem, o_sem, ag_s, ag_r, rs_s, rs_r, is_s, is_r,
):
    isl = lax.axis_index("island")
    f = lax.axis_index("fsdp")
    x = f // 16
    z = (f // 4) % 4
    y = f % 4
    xl = isl // 2
    core = isl % 2

    def at(xx, zz, yy):
        return (isl, xx * 16 + zz * 4 + yy)

    up = lambda m: (m + 1) % 4
    down = lambda m: (m + 3) % 4
    opposite = lambda m: (m + 2) % 4
    ydev = (at(x, z, up(y)), at(x, z, down(y)))
    zdev = (at(x, up(z), y), at(x, down(z), y))
    xdev = at(1 - x, z, y)
    isl_core = xl * 2 + (1 - core)
    isl_x = (1 - xl) * 2 + core
    isl_far = 3 - isl
    cdev = (isl_core, f)
    ldev = (isl_x, f)

    own_copy = pltpu.make_async_copy(
        tok_hbm.at[0], toks.at[x, z, pl.ds(pl.multiple_of(y * OWN, OWN), OWN), :], l_sem.at[0]
    )
    own_copy.start()
    w_copies = []
    for p in range(NP):
        rows = pl.ds(p * PC, PC)
        pair = []
        for j, src in enumerate((wg_hbm, wu_hbm)):
            copy = pltpu.make_async_copy(
                src.at[0, rows, :], wts.at[rows, pl.ds(j * HID, HID)], w_sem.at[p, j]
            )
            copy.start()
            pair.append(copy)
        w_copies.append(pair)
    dh_copy = pltpu.make_async_copy(dh_hbm.at[0], dhid, l_sem.at[1])
    dh_copy.start()

    barrier = pltpu.get_barrier_semaphore()
    for dev in (*ydev, *zdev, xdev, cdev, ldev):
        pl.semaphore_signal(barrier, inc=1, device_id=dev, device_id_type=MESH)

    def hot(p, _):
        lo = pl.multiple_of(p * 256, 256)
        down_rows = lax.broadcasted_iota(jnp.int32, (256, FRAG), 0) + lo
        oh[pl.ds(lo, 256), :] = jnp.where(down_rows == row_ref[...], 1.0, 0.0).astype(BF)
        along = lax.broadcasted_iota(jnp.int32, (FRAG, 256), 1) + lo
        oht[:, pl.ds(lo, 256)] = jnp.where(along == col_ref[...], 1.0, 0.0).astype(BF)
        return 0

    lax.fori_loop(0, D // 256, hot, 0)
    pl.semaphore_wait(barrier, 7)

    started = []

    def send(src, dst, ss, rs, dev):
        copy = pltpu.make_async_remote_copy(
            src_ref=src, dst_ref=dst, send_sem=ss, recv_sem=rs, device_id=dev, device_id_type=MESH
        )
        copy.start()
        started.append(copy)

    def arrived(ref, rs, ss):
        pltpu.make_async_remote_copy(
            src_ref=ref, dst_ref=ref, send_sem=ss, recv_sem=rs, device_id=xdev, device_id_type=MESH
        ).wait_recv()

    def ysl(m):
        return pl.ds(pl.multiple_of(m * OWN, OWN), OWN)

    def cols_of(c, half=None):
        if half is None:
            return pl.ds(c * DC, DC)
        return pl.ds(c * DC + half * HC, HC)

    def first_part(c, m, half=None):
        if c % 2 == 0:
            return toks.at[:, z, ysl(m), cols_of(c, half)]
        return toks.at[:, m, ysl(y), cols_of(c, half)]

    def second_part(c, m, half=None):
        if c % 2 == 0:
            return toks.at[:, m, :, cols_of(c, half)]
        return toks.at[:, :, ysl(m), cols_of(c, half)]

    def ring_send(c, part_of, m, dev, k):
        for j in range(2):
            send(part_of(c, m), part_of(c, m), ag_s.at[c, k + j], ag_r.at[c, k + j], dev[j])

    def ring_relay(c, part_of, m, dev, k):
        for j, near in enumerate((down(m), up(m))):
            arrived(part_of(c, near), ag_r.at[c, k + j], ag_s.at[c, k + j])
            piece = part_of(c, near, j)
            send(piece, piece, ag_s.at[c, k + 2 + j], ag_r.at[c, k + 2 + j], dev[j])

    def ring_end(c, part_of, m, k):
        for j in range(2):
            arrived(part_of(c, opposite(m), j), ag_r.at[c, k + 2 + j], ag_s.at[c, k + 2 + j])

    def axes(c):
        return ((y, ydev), (z, zdev)) if c % 2 == 0 else ((z, zdev), (y, ydev))

    for c in range(NC):
        send(
            tok_hbm.at[0, :, cols_of(c)],
            toks.at[x, z, ysl(y), cols_of(c)],
            ag_s.at[c, 0], ag_r.at[c, 0], xdev,
        )
    own_copy.wait()
    for c in range(NC):
        arrived(toks.at[1 - x, z, ysl(y), cols_of(c)], ag_r.at[c, 0], ag_s.at[c, 0])
        (m1, dev1), _ = axes(c)
        ring_send(c, first_part, m1, dev1, 1)

    def ncols(n):
        return pl.ds(pl.multiple_of(n * 256, 256), 256)

    def pick_rows(p):
        for copy in w_copies[p]:
            copy.wait()

        def body(n, _):
            value = jnp.dot(
                oht[:, p * PC:(p + 1) * PC], wts[pl.ds(p * PC, PC), ncols(n)],
                preferred_element_type=F32,
            )
            if p > 0:
                value = value + rowp[:, ncols(n)]
            rowp[:, ncols(n)] = value
            return 0

        lax.fori_loop(0, W2 // 256, body, 0)

    for p in range(NP):
        for c in (2 * p, 2 * p + 1):
            (m1, dev1), _ = axes(c)
            ring_relay(c, first_part, m1, dev1, 1)
        pick_rows(p)

    def forward(p):
        def body(n, _):
            value = jnp.dot(
                toks[:, :, :, p * PC:(p + 1) * PC].reshape(TOK, PC),
                wts[pl.ds(p * PC, PC), ncols(n)],
                preferred_element_type=F32,
            )
            if p > 0:
                value = value + acc[:, ncols(n)]
            acc[:, ncols(n)] = value
            return 0

        lax.fori_loop(0, W2 // 256, body, 0)
        value = jnp.dot(
            toks[:, :, :, p * PC:(p + 1) * PC].reshape(TOK, PC),
            oh[p * PC:(p + 1) * PC, :],
            preferred_element_type=F32,
        )
        if p > 0:
            value = value + pick[...]
        pick[...] = value

    for t in range(NP + 2):
        if t < NP:
            for c in (2 * t, 2 * t + 1):
                (m1, _), (m2, dev2) = axes(c)
                ring_end(c, first_part, m1, 1)
                ring_send(c, second_part, m2, dev2, 5)
        if 0 <= t - 1 < NP:
            for c in (2 * t - 2, 2 * t - 1):
                _, (m2, dev2) = axes(c)
                ring_relay(c, second_part, m2, dev2, 5)
        if t == 0:
            rows_all[isl] = rowp[...].astype(BF)
            send(rows_all.at[isl], rows_all.at[isl], is_s.at[0], is_r.at[0], cdev)
            send(rows_all.at[isl], rows_all.at[isl], is_s.at[1], is_r.at[1], ldev)
        if t >= 2:
            for c in (2 * t - 4, 2 * t - 3):
                _, (m2, _) = axes(c)
                ring_end(c, second_part, m2, 5)
            forward(t - 2)

    dh_copy.wait()

    def gated(r, _):
        rr = pl.ds(pl.multiple_of(r * 16, 16), 16)
        gate = acc[rr, 0:HID] * FACTOR
        upv = acc[rr, HID:W2] * FACTOR
        g = dhid[rr, :].astype(F32)
        s = jax.nn.sigmoid(gate)
        dcat[rr, 0:HID] = (g * upv * (s * (1.0 + gate * (1.0 - s)))).astype(BF)
        dcat[rr, HID:W2] = (g * (gate * s)).astype(BF)
        return 0

    lax.fori_loop(0, TOK // 16, gated, 0)

    def backward(c):
        for n in range(DC // 256):
            lo = c * DC + n * 256
            value = lax.dot_general(
                dcat[...], wts[pl.ds(lo, 256), :], (((1,), (1,)), ((), ())),
                preferred_element_type=F32,
            )
            part[:, :, :, lo:lo + 256] = value.reshape(2, 4, 64, 256)

    def block1(c, m, half=None):
        if c % 2 == 0:
            return part[:, m, :, cols_of(c, half)].reshape(128, DC if half is None else HC)
        return part[:, :, ysl(m), cols_of(c, half)].reshape(128, DC if half is None else HC)

    def block2(c, m, half=None):
        if half is None:
            return quart[c, :, m].reshape(32, DC)
        return quart[c, :, m, :, half * HC:(half + 1) * HC].reshape(32, HC)

    def far_out(c, block, m, dev, sb, rb, k):
        sb[c, 0] = block(c, opposite(m)).astype(BF)
        for j in range(2):
            hs = pl.ds(j * HC, HC)
            send(sb.at[c, 0, :, hs], rb.at[c, 0, :, hs], rs_s.at[c, k + j], rs_r.at[c, k + j], dev[j])

    def near_out(c, block, m, dev, sb, rb, k):
        for j, near in enumerate((up(m), down(m))):
            hs = pl.ds(j * HC, HC)
            ot = pl.ds((1 - j) * HC, HC)
            sb[c, 1 + j, :, ot] = block(c, near, 1 - j).astype(BF)
            arrived(rb.at[c, 0, :, hs], rs_r.at[c, k + j], rs_s.at[c, k + j])
            sb[c, 1 + j, :, hs] = (block(c, near, j) + rb[c, 0, :, hs].astype(F32)).astype(BF)
            send(
                sb.at[c, 1 + j], rb.at[c, 1 + j], rs_s.at[c, k + 2 + j], rs_r.at[c, k + 2 + j], dev[j]
            )

    def total(c, block, m, rb, k):
        for j in range(2):
            arrived(rb.at[c, 1 + j], rs_r.at[c, k + 2 + j], rs_s.at[c, k + 2 + j])
        return block(c, m) + (rb[c, 1].astype(F32) + rb[c, 2].astype(F32))

    def scatter_axes(c):
        return ((z, zdev), (y, ydev)) if c % 2 == 0 else ((y, ydev), (z, zdev))

    def gradient():
        pk = jnp.transpose(pick[...]).astype(BF)

        def body(n, _):
            gradv[:, ncols(n)] = (
                jnp.dot(pk, dcat[:, ncols(n)], preferred_element_type=F32) * FACTOR
            )
            return 0

        lax.fori_loop(0, W2 // 256, body, 0)

    grad_copy = pltpu.make_async_copy(gradv, grad_hbm, o_sem.at[0])
    rsum_copy = pltpu.make_async_copy(rsumv, rsum_hbm, o_sem.at[1])
    dtok_copy = pltpu.make_async_copy(dtokv, dtok_hbm, o_sem.at[2])

    for t in range(NP + 5):
        if t < NP:
            for c in (2 * t, 2 * t + 1):
                (m1, dev1), _ = scatter_axes(c)
                backward(c)
                far_out(c, block1, m1, dev1, sb1, rb1, 0)
        if 0 <= t - 1 < NP:
            for c in (2 * t - 2, 2 * t - 1):
                (m1, dev1), _ = scatter_axes(c)
                near_out(c, block1, m1, dev1, sb1, rb1, 0)
        if 0 <= t - 2 < NP:
            for c in (2 * t - 4, 2 * t - 3):
                (m1, _), (m2, dev2) = scatter_axes(c)
                quart[c] = total(c, block1, m1, rb1, 0).reshape(2, 4, OWN, DC)
                far_out(c, block2, m2, dev2, sb2, rb2, 4)
        if 0 <= t - 3 < NP:
            for c in (2 * t - 6, 2 * t - 5):
                _, (m2, dev2) = scatter_axes(c)
                near_out(c, block2, m2, dev2, sb2, rb2, 4)
        if 0 <= t - 4 < NP:
            for c in (2 * t - 8, 2 * t - 7):
                _, (m2, _) = scatter_axes(c)
                last[c] = total(c, block2, m2, rb2, 4).reshape(2, OWN, DC)
                sbx[c] = last[c, 1 - x].astype(BF)
                send(sbx.at[c], rbx.at[c], rs_s.at[c, 8], rs_r.at[c, 8], xdev)
        if t >= 5:
            for c in (2 * t - 10, 2 * t - 9):
                arrived(rbx.at[c], rs_r.at[c, 8], rs_s.at[c, 8])
                dtokv[:, cols_of(c)] = ((last[c, x] + rbx[c].astype(F32)) * FACTOR).astype(BF)
        if t == 1:
            gradient()
            grad_copy.start()
            arrived(rows_all.at[isl_x], is_r.at[1], is_s.at[1])
            send(rows_all.at[isl_x], rows_all.at[isl_x], is_s.at[2], is_r.at[2], cdev)
        if t == 2:
            arrived(rows_all.at[isl_core], is_r.at[0], is_s.at[0])
            arrived(rows_all.at[isl_far], is_r.at[2], is_s.at[2])

            def add_rows(r, _):
                rr = pl.ds(pl.multiple_of(r * 16, 16), 16)
                tot = rows_all[0, rr, :].astype(F32)
                for k in range(1, 4):
                    tot = tot + rows_all[k, rr, :].astype(F32)
                rsumv[rr, :] = tot
                return 0

            lax.fori_loop(0, FRAG // 16, add_rows, 0)
            rsum_copy.start()

    dtok_copy.start()
    for copy in started:
        copy.wait_send()
    grad_copy.wait()
    rsum_copy.wait()
    dtok_copy.wait()


def exchange(tokens, w_gate, w_up, d_hidden, fragment_rows):
    any_spec = pl.BlockSpec(memory_space=pl.ANY)
    vmem = pl.BlockSpec(memory_space=pltpu.VMEM)
    dma = pltpu.SemaphoreType.DMA
    return pl.pallas_call(
        step_kernel,
        out_shape=(
            jax.ShapeDtypeStruct((OWN, D), BF),
            jax.ShapeDtypeStruct((FRAG, W2), F32),
            jax.ShapeDtypeStruct((FRAG, W2), F32),
        ),
        in_specs=[any_spec] * 4 + [vmem] * 2,
        out_specs=(any_spec,) * 3,
        scratch_shapes=[
            pltpu.VMEM((D, W2), BF),
            pltpu.VMEM((2, 4, 64, D), BF),
            pltpu.VMEM((TOK, W2), F32),
            pltpu.VMEM((TOK, W2), BF),
            pltpu.VMEM((TOK, HID), BF),
            pltpu.VMEM((2, 4, 64, D), F32),
            pltpu.VMEM((D, FRAG), BF),
            pltpu.VMEM((FRAG, D), BF),
            pltpu.VMEM((TOK, FRAG), F32),
            pltpu.VMEM((FRAG, W2), F32),
            pltpu.VMEM((4, FRAG, W2), BF),
            pltpu.VMEM((FRAG, W2), F32),
            pltpu.VMEM((FRAG, W2), F32),
            pltpu.VMEM((OWN, D), BF),
            pltpu.VMEM((NC, 3, 128, DC), BF),
            pltpu.VMEM((NC, 3, 128, DC), BF),
            pltpu.VMEM((NC, 3, 32, DC), BF),
            pltpu.VMEM((NC, 3, 32, DC), BF),
            pltpu.VMEM((NC, 2, 4, OWN, DC), F32),
            pltpu.VMEM((NC, 2, OWN, DC), F32),
            pltpu.VMEM((NC, OWN, DC), BF),
            pltpu.VMEM((NC, OWN, DC), BF),
            dma((NP, 2)),
            dma((2,)),
            dma((3,)),
            dma((NC, AG)),
            dma((NC, AG)),
            dma((NC, RS)),
            dma((NC, RS)),
            dma((3,)),
            dma((3,)),
        ],
        compiler_params=pltpu.CompilerParams(
            collective_id=0, has_side_effects=True, vmem_limit_bytes=60 * 2**20
        ),
        cost_estimate=pl.CostEstimate(
            flops=16 * 10**9, bytes_accessed=18 * 10**6, transcendentals=TOK * HID
        ),
        name="gather_compute_scatter",
    )(tokens, w_gate, w_up, d_hidden, fragment_rows.reshape(1, FRAG), fragment_rows.reshape(FRAG, 1))


def adam_kernel(
    dtok, grad, rsum, outer, mom, first, second,
    dtok_out, frag_out, outer_out, mom_out, first_out, second_out,
):
    dtok_out[0] = dtok[...]
    g = grad[...]
    o = outer[0]
    mean_delta = o - rsum[...] * 0.25
    m = 0.9 * mom[0] + mean_delta
    on = o - 0.7 * (mean_delta + 0.9 * m)
    f = 0.9 * first[0, 0] + 0.1 * g
    s = 0.95 * second[0, 0] + 0.05 * (g * g)
    mom_out[0] = m
    outer_out[0] = on
    first_out[0, 0] = f
    second_out[0, 0] = s
    frag_out[0, 0] = (on * (1.0 - 0.02 * 0.1) - 0.02 * f / (jnp.sqrt(s) + 1e-08)).astype(BF)


def update(dtok, grad, rsum, outer, mom, first, second):
    rows = 32
    whole = pl.BlockSpec((OWN, D), lambda j, k: (0, 0))
    whole_out = pl.BlockSpec((1, OWN, D), lambda j, k: (0, 0, 0))
    flat = pl.BlockSpec((rows, HID), lambda j, k: (k, j))
    three = pl.BlockSpec((1, rows, HID), lambda j, k: (j, k, 0))
    four = pl.BlockSpec((1, 1, rows, HID), lambda j, k: (0, j, k, 0))
    return pl.pallas_call(
        adam_kernel,
        grid=(2, FRAG // rows),
        out_shape=(
            jax.ShapeDtypeStruct((1, OWN, D), BF),
            jax.ShapeDtypeStruct((1, 2, FRAG, HID), BF),
            jax.ShapeDtypeStruct((2, FRAG, HID), F32),
            jax.ShapeDtypeStruct((2, FRAG, HID), F32),
            jax.ShapeDtypeStruct((1, 2, FRAG, HID), F32),
            jax.ShapeDtypeStruct((1, 2, FRAG, HID), F32),
        ),
        in_specs=[whole, flat, flat, three, three, four, four],
        out_specs=(whole_out, four, three, three, four, four),
        name="update",
    )(dtok, grad, rsum, outer, mom, first, second)


def per_device(
    tokens, w_gate, w_up, d_hidden, outer_rows, outer_momentum, adam_first, adam_second, fragment_rows
):
    dtok, grad, rsum = exchange(tokens, w_gate, w_up, d_hidden, fragment_rows)
    return update(dtok, grad, rsum, outer_rows, outer_momentum, adam_first, adam_second)


def solution(mesh):
    return jax.shard_map(
        per_device,
        mesh=mesh,
        in_specs=(
            P("island", "fsdp", None),
            P("island", None, "fsdp"),
            P("island", None, "fsdp"),
            P("island", None, "fsdp"),
            P(None, None, "fsdp"),
            P(None, None, "fsdp"),
            P("island", None, None, "fsdp"),
            P("island", None, None, "fsdp"),
            P(),
        ),
        out_specs=(
            P("island", "fsdp", None),
            P("island", None, None, "fsdp"),
            P(None, None, "fsdp"),
            P(None, None, "fsdp"),
            P("island", None, None, "fsdp"),
            P("island", None, None, "fsdp"),
        ),
        check_vma=False,
    )
```

```python
import jax
import jax.numpy as jnp
from jax import lax
from jax.experimental import pallas as pl
from jax.experimental.pallas import tpu as pltpu
from jax.sharding import PartitionSpec as P

MESH = pl.DeviceIdType.MESH
BF = jnp.bfloat16
F32 = jnp.float32

D = 4096
HID = 896
W2 = 2 * HID
TOK = 512
OWN = 16
FRAG = 128
CHUNKS = ((0, 768), (768, 768), (1536, 768), (2304, 768), (3072, 512), (3584, 512))
NC = len(CHUNKS)
ND = 4
WIDE = 768
DW = 512
GATHER = (((0, 4), (0, 5)), ((0, 0), (0, 1)), ((0, 2), (0, 3)), ((1, 0), (1, 1)), ((1, 2), (1, 3)))
SCATTER = (((0, 0), (0, 1)), ((0, 2), (0, 3)), ((1, 0), (1, 1)), ((1, 2), (1, 3)), ((0, 4), (0, 5)))
T = len(GATHER)
HALF = TOK // 2
FACTOR = float(D) ** (-0.5)
NW = 4
WC = D // NW
MSG = 9
VMEM_GRANT = 55 * 2**20
DECAY = 1.0 - 0.02 * 0.1


def step_kernel(
    tok_hbm, wg_hbm, wu_hbm, dh_hbm, outer_hbm, mom_hbm, first_hbm, second_hbm, row_ref,
    dtokv, fragv, outerv, momv, firstv, secondv,
    wts, toks, acc, dcat, dhid, part, oh, oht, pick, rowp, rows_all,
    sb1, rb1, sb2, rb2, quart, sbx, rbx, sbd, rbd, own_sum,
    w_sem, l_sem, ag_s, ag_r, rs_s, rs_r, is_s, is_r,
):
    isl = lax.axis_index("island")
    f = lax.axis_index("fsdp")
    x = f // 16
    z = (f // 4) % 4
    y = f % 4
    xl = isl // 2
    core = isl % 2

    def at(xx, zz, yy):
        return (isl, xx * 16 + zz * 4 + yy)

    def up(m):
        return (m + 1) % 4

    def down(m):
        return (m + 3) % 4

    def opposite(m):
        return (m + 2) % 4

    ydev = (at(x, z, up(y)), at(x, z, down(y)), at(x, z, opposite(y)))
    zdev = (at(x, up(z), y), at(x, down(z), y), at(x, opposite(z), y))
    xdev = at(1 - x, z, y)
    isl_core = xl * 2 + (1 - core)
    isl_x = (1 - xl) * 2 + core
    isl_far = 3 - isl
    cdev = (isl_core, f)
    ldev = (isl_x, f)

    def ysl(m):
        return pl.ds(pl.multiple_of(m * OWN, OWN), OWN)

    own_copy = pltpu.make_async_copy(tok_hbm.at[0], toks.at[0, z, ysl(y), :], l_sem.at[0])
    own_copy.start()
    w_copies = []
    for p in range(NW):
        rows = pl.ds(p * WC, WC)
        pair = []
        for j, src in enumerate((wg_hbm, wu_hbm)):
            copy = pltpu.make_async_copy(
                src.at[0, rows, :], wts.at[rows, pl.ds(j * HID, HID)], w_sem.at[p, j]
            )
            copy.start()
            pair.append(copy)
        w_copies.append(pair)
    dh_copies = []
    for h, plane in ((0, x), (1, 1 - x)):
        rows = pl.ds(pl.multiple_of(plane * HALF, HALF), HALF)
        copy = pltpu.make_async_copy(dh_hbm.at[0, rows, :], dhid.at[h], l_sem.at[1 + h])
        copy.start()
        dh_copies.append(copy)
    state_copies = []
    for k, (src, dst) in enumerate(
        ((outer_hbm, outerv), (mom_hbm, momv), (first_hbm, firstv), (second_hbm, secondv))
    ):
        copy = pltpu.make_async_copy(src, dst, l_sem.at[3 + k])
        copy.start()
        state_copies.append(copy)

    barrier = pltpu.get_barrier_semaphore()
    greeted = (*ydev, *zdev, xdev, cdev, ldev)
    for dev in greeted:
        pl.semaphore_signal(barrier, inc=1, device_id=dev, device_id_type=MESH)

    spread = jnp.transpose(jnp.broadcast_to(row_ref[...], (FRAG, FRAG)))

    def hot(p, _):
        lo = pl.multiple_of(p * 128, 128)
        down_rows = lax.broadcasted_iota(jnp.int32, (128, FRAG), 0) + lo
        oh[pl.ds(lo, 128), :] = jnp.where(down_rows == row_ref[...], 1.0, 0.0).astype(BF)
        along = lax.broadcasted_iota(jnp.int32, (FRAG, 128), 1) + lo
        oht[:, pl.ds(lo, 128)] = jnp.where(along == spread, 1.0, 0.0).astype(BF)
        return 0

    pl.semaphore_wait(barrier, len(greeted))

    started = []

    def send(src, dst, ss, rs, dev):
        copy = pltpu.make_async_remote_copy(
            src_ref=src, dst_ref=dst, send_sem=ss, recv_sem=rs, device_id=dev, device_id_type=MESH
        )
        copy.start()
        started.append(copy)

    def arrived(ref, rs, ss):
        pltpu.make_async_remote_copy(
            src_ref=ref, dst_ref=ref, send_sem=ss, recv_sem=rs, device_id=xdev, device_id_type=MESH
        ).wait_recv()

    def cols_of(c, half=None):
        lo, w = CHUNKS[c]
        if half is None:
            return pl.ds(lo, w)
        return pl.ds(lo + half * (w // 2), w // 2)

    def axes(c):
        return ((y, ydev), (z, zdev)) if c % 2 == 0 else ((z, zdev), (y, ydev))

    def own_part(h, c, m):
        if c % 2 == 0:
            return toks.at[h, z, ysl(m), cols_of(c)]
        return toks.at[h, m, ysl(y), cols_of(c)]

    def ring_part(h, c, m, half=None):
        if c % 2 == 0:
            return toks.at[h, m, :, cols_of(c, half)]
        return toks.at[h, :, ysl(m), cols_of(c, half)]

    def spread_own(h, c):
        (m, dev), _ = axes(c)
        for j in range(3):
            piece = own_part(h, c, m)
            source = tok_hbm.at[0, :, cols_of(c)] if h == 0 else piece
            send(source, piece, ag_s.at[h, c, 1 + j], ag_r.at[h, c, 1 + j], dev[j])

    def spread_end(h, c):
        (m, _), _ = axes(c)
        for j, other in enumerate((down(m), up(m), opposite(m))):
            arrived(own_part(h, c, other), ag_r.at[h, c, 1 + j], ag_s.at[h, c, 1 + j])

    def ring_send(h, c):
        _, (m, dev) = axes(c)
        for j in range(2):
            piece = ring_part(h, c, m)
            send(piece, piece, ag_s.at[h, c, 5 + j], ag_r.at[h, c, 5 + j], dev[j])

    def ring_relay(h, c):
        _, (m, dev) = axes(c)
        for j, near in enumerate((down(m), up(m))):
            arrived(ring_part(h, c, near), ag_r.at[h, c, 5 + j], ag_s.at[h, c, 5 + j])
            piece = ring_part(h, c, near, j)
            send(piece, piece, ag_s.at[h, c, 7 + j], ag_r.at[h, c, 7 + j], dev[j])

    def ring_end(h, c):
        _, (m, _) = axes(c)
        for j in range(2):
            arrived(ring_part(h, c, opposite(m), j), ag_r.at[h, c, 7 + j], ag_s.at[h, c, 7 + j])

    for pair in GATHER[:3]:
        for h, c in pair:
            spread_own(h, c)
    for c in range(ND):
        send(
            tok_hbm.at[0, :, cols_of(c)], toks.at[1, z, ysl(y), cols_of(c)],
            ag_s.at[1, c, 0], ag_r.at[1, c, 0], xdev,
        )
    lax.fori_loop(0, D // 128, hot, 0)
    own_copy.wait()

    def spread_partner():
        for c in range(ND):
            arrived(toks.at[1, z, ysl(y), cols_of(c)], ag_r.at[1, c, 0], ag_s.at[1, c, 0])
            spread_own(1, c)

    def direct_send(c):
        send(
            toks.at[0, :, :, cols_of(c)], toks.at[1, :, :, cols_of(c)],
            ag_s.at[1, c, 0], ag_r.at[1, c, 0], xdev,
        )

    def direct_end(c):
        arrived(toks.at[1, :, :, cols_of(c)], ag_r.at[1, c, 0], ag_s.at[1, c, 0])

    def pick_rows(p):
        for copy in w_copies[p]:
            copy.wait()
        value = jnp.dot(
            oht[:, p * WC:(p + 1) * WC], wts[p * WC:(p + 1) * WC, :], preferred_element_type=F32
        )
        rowp[...] = value if p == 0 else value + rowp[...]

    def pick_all(lo, hi):
        for p in range(lo, hi):
            pick_rows(p)

    def share_rows():
        rows_all[isl] = rowp[...].astype(BF)
        send(rows_all.at[isl], rows_all.at[isl], is_s.at[0], is_r.at[0], cdev)
        send(rows_all.at[isl], rows_all.at[isl], is_s.at[1], is_r.at[1], ldev)

    def forward(h, c, start):
        lo, w = CHUNKS[c]
        hi = lo + w
        lhs = toks[h, :, :, lo:hi].reshape(HALF, w)
        value = jnp.dot(lhs, wts[lo:hi, :], preferred_element_type=F32)
        acc[h] = value if start else value + acc[h]
        value = jnp.dot(lhs, oh[lo:hi, :], preferred_element_type=F32)
        pick[h] = value if start else value + pick[h]

    def gated(h):
        dh_copies[h].wait()

        def body(r, _):
            rr = pl.ds(pl.multiple_of(r * 16, 16), 16)
            gate = acc[h, rr, 0:HID] * FACTOR
            upv = acc[h, rr, HID:W2] * FACTOR
            g = dhid[h, rr, :].astype(F32)
            s = jax.nn.sigmoid(gate)
            dcat[h, rr, 0:HID] = (g * upv * (s * (1.0 + gate * (1.0 - s)))).astype(BF)
            dcat[h, rr, HID:W2] = (g * (gate * s)).astype(BF)
            return 0

        lax.fori_loop(0, HALF // 16, body, 0)

    def backward(h, c):
        lo, w = CHUNKS[c]
        hi = lo + w
        value = lax.dot_general(
            dcat[h], wts[lo:hi, :], (((1,), (1,)), ((), ())), preferred_element_type=F32
        )
        if h == 1 and c >= ND:
            sbd[c - ND] = value.reshape(4, 64, w).astype(BF)
            send(sbd.at[c - ND], rbd.at[c - ND], rs_s.at[h, c, 8], rs_r.at[h, c, 8], xdev)
            return
        value = value.reshape(4, 64, w)
        if c >= ND:
            arrived(rbd.at[c - ND], rs_r.at[1, c, 8], rs_s.at[1, c, 8])
            value = value + rbd[c - ND].astype(F32)
        part[h, :, :, lo:hi] = value

    def scatter_axes(c):
        return ((z, zdev), (y, ydev)) if c % 2 == 0 else ((y, ydev), (z, zdev))

    def block1(h, c, m, half=None):
        if c % 2 == 0:
            return part[h, m, :, cols_of(c, half)]
        w = CHUNKS[c][1]
        return part[h, :, ysl(m), cols_of(c, half)].reshape(64, w if half is None else w // 2)

    def wide(c):
        return pl.ds(0, CHUNKS[c][1])

    def halves(c, j):
        w = CHUNKS[c][1] // 2
        return pl.ds(j * w, w)

    def far_out(h, c):
        (m, dev), _ = scatter_axes(c)
        sb1[h, c, 0, :, wide(c)] = block1(h, c, opposite(m)).astype(BF)
        for j in range(2):
            hs = halves(c, j)
            send(
                sb1.at[h, c, 0, :, hs], rb1.at[h, c, 0, :, hs],
                rs_s.at[h, c, j], rs_r.at[h, c, j], dev[j],
            )

    def near_out(h, c):
        (m, dev), _ = scatter_axes(c)
        for j, near in enumerate((up(m), down(m))):
            hs = halves(c, j)
            ot = halves(c, 1 - j)
            sb1[h, c, 1 + j, :, ot] = block1(h, c, near, 1 - j).astype(BF)
            arrived(rb1.at[h, c, 0, :, hs], rs_r.at[h, c, j], rs_s.at[h, c, j])
            sb1[h, c, 1 + j, :, hs] = (
                block1(h, c, near, j) + rb1[h, c, 0, :, hs].astype(F32)
            ).astype(BF)
            send(
                sb1.at[h, c, 1 + j, :, wide(c)], rb1.at[h, c, 1 + j, :, wide(c)],
                rs_s.at[h, c, 2 + j], rs_r.at[h, c, 2 + j], dev[j],
            )

    def ring_total(h, c):
        w = wide(c)
        (m, _), (m2, dev2) = scatter_axes(c)
        for j in range(2):
            arrived(rb1.at[h, c, 1 + j, :, w], rs_r.at[h, c, 2 + j], rs_s.at[h, c, 2 + j])
        value = block1(h, c, m) + (
            rb1[h, c, 1, :, w].astype(F32) + rb1[h, c, 2, :, w].astype(F32)
        )
        quart[h, c, :, :, w] = value.reshape(4, OWN, CHUNKS[c][1])
        for j, other in enumerate((up(m2), down(m2), opposite(m2))):
            sb2[h, c, j, :, w] = quart[h, c, other, :, w].astype(BF)
            send(
                sb2.at[h, c, j, :, w], rb2.at[h, c, j, :, w],
                rs_s.at[h, c, 4 + j], rs_r.at[h, c, 4 + j], dev2[j],
            )

    def plane_total(h, c):
        w = wide(c)
        _, (m2, _) = scatter_axes(c)
        for j in range(3):
            arrived(rb2.at[h, c, j, :, w], rs_r.at[h, c, 4 + j], rs_s.at[h, c, 4 + j])
        value = quart[h, c, m2, :, w] + (
            (rb2[h, c, 0, :, w].astype(F32) + rb2[h, c, 1, :, w].astype(F32))
            + rb2[h, c, 2, :, w].astype(F32)
        )
        if h == 1:
            sbx[c] = value.astype(BF)
            send(sbx.at[c], rbx.at[c], rs_s.at[h, c, 8], rs_r.at[h, c, 8], xdev)
        elif c < ND:
            own_sum[:, cols_of(c)] = value
        else:
            dtokv[:, cols_of(c)] = (value * FACTOR).astype(BF)

    def finish(c):
        arrived(rbx.at[c], rs_r.at[1, c, 8], rs_s.at[1, c, 8])
        value = own_sum[:, cols_of(c)] + rbx[c].astype(F32)
        dtokv[:, cols_of(c)] = (value * FACTOR).astype(BF)

    def gradient():
        pk = jnp.transpose(pick[...].reshape(TOK, FRAG)).astype(BF)
        acc[0, 0:FRAG, :] = (
            jnp.dot(pk, dcat[...].reshape(TOK, W2), preferred_element_type=F32) * FACTOR
        )

    def pass_rows():
        arrived(rows_all.at[isl_x], is_r.at[1], is_s.at[1])
        send(rows_all.at[isl_x], rows_all.at[isl_x], is_s.at[2], is_r.at[2], cdev)

    def optimize():
        arrived(rows_all.at[isl_core], is_r.at[0], is_s.at[0])
        arrived(rows_all.at[isl_far], is_r.at[2], is_s.at[2])
        for copy in state_copies:
            copy.wait()

        def body(i, _):
            rr = pl.ds(pl.multiple_of(i * 16, 16), 16)
            for j in range(2):
                cols = pl.ds(j * HID, HID)
                rsum = rows_all[0, rr, cols].astype(F32)
                for k in range(1, 4):
                    rsum = rsum + rows_all[k, rr, cols].astype(F32)
                outer = outerv[j, rr]
                g = acc[0, rr, cols]
                mean_delta = outer - rsum * 0.25
                mom = 0.9 * momv[j, rr] + mean_delta
                outer = outer - 0.7 * (mean_delta + 0.9 * mom)
                first = 0.9 * firstv[0, j, rr] + 0.1 * g
                second = 0.95 * secondv[0, j, rr] + 0.05 * (g * g)
                momv[j, rr] = mom
                outerv[j, rr] = outer
                firstv[0, j, rr] = first
                secondv[0, j, rr] = second
                fragv[0, j, rr] = (
                    outer * DECAY - 0.02 * first / (jnp.sqrt(second) + 1e-08)
                ).astype(BF)
            return 0

        lax.fori_loop(0, FRAG // 16, body, 0)

    for s in range(2 * T + 4):
        if s < T:
            for item in GATHER[s]:
                spread_end(*item)
                ring_send(*item)
        if s == 0:
            spread_partner()
            pick_all(0, NW // 2)
        if 0 <= s - 1 < T:
            for item in GATHER[s - 1]:
                ring_relay(*item)
        if s == 1:
            pick_all(NW // 2, NW)
        r = s - T
        if 0 <= r < T:
            if r == 2:
                for c in range(ND, NC):
                    backward(1, c)
            for item in SCATTER[r]:
                backward(*item)
                far_out(*item)
        if 0 <= r - 1 < T:
            for item in SCATTER[r - 1]:
                near_out(*item)
        if 0 <= r - 2 < T:
            for item in SCATTER[r - 2]:
                ring_total(*item)
        if 0 <= r - 3 < T:
            for item in SCATTER[r - 3]:
                plane_total(*item)
        if r == 0:
            share_rows()
        if r == 3:
            pass_rows()
            gradient()
        if r == 4:
            optimize()
        if 0 <= s - 2 < T:
            for h, c in GATHER[s - 2]:
                ring_end(h, c)
                if h == 0 and c >= ND:
                    direct_send(c)
                forward(h, c, s == 2 and c == ND or s == 5 and c == 0)
            if s == 4:
                gated(0)
            if s == 6:
                for c in range(ND, NC):
                    direct_end(c)
                    forward(1, c, False)
                gated(1)
    for c in range(ND):
        finish(c)

    for copy in started:
        copy.wait_send()


STATE = (
    jax.ShapeDtypeStruct((1, OWN, D), BF),
    jax.ShapeDtypeStruct((1, 2, FRAG, HID), BF),
    jax.ShapeDtypeStruct((2, FRAG, HID), F32),
    jax.ShapeDtypeStruct((2, FRAG, HID), F32),
    jax.ShapeDtypeStruct((1, 2, FRAG, HID), F32),
    jax.ShapeDtypeStruct((1, 2, FRAG, HID), F32),
)


def exchange(*args):
    any_spec = pl.BlockSpec(memory_space=pl.ANY)
    vmem = pl.BlockSpec(memory_space=pltpu.VMEM)
    dma = pltpu.SemaphoreType.DMA
    *arrays, fragment_rows = args
    return pl.pallas_call(
        step_kernel,
        out_shape=tuple(pltpu.VMEM(s.shape, s.dtype) for s in (jax.ShapeDtypeStruct((OWN, D), BF),) + STATE[1:]),
        in_specs=[any_spec] * 8 + [vmem],
        out_specs=(vmem,) * 6,
        scratch_shapes=[
            pltpu.VMEM((D, W2), BF),
            pltpu.VMEM((2, 4, 64, D), BF),
            pltpu.VMEM((2, HALF, W2), F32),
            pltpu.VMEM((2, HALF, W2), BF),
            pltpu.VMEM((2, HALF, HID), BF),
            pltpu.VMEM((2, 4, 64, D), F32),
            pltpu.VMEM((D, FRAG), BF),
            pltpu.VMEM((FRAG, D), BF),
            pltpu.VMEM((2, HALF, FRAG), F32),
            pltpu.VMEM((FRAG, W2), F32),
            pltpu.VMEM((4, FRAG, W2), BF),
            pltpu.VMEM((2, NC, 3, 64, WIDE), BF),
            pltpu.VMEM((2, NC, 3, 64, WIDE), BF),
            pltpu.VMEM((2, NC, 3, OWN, WIDE), BF),
            pltpu.VMEM((2, NC, 3, OWN, WIDE), BF),
            pltpu.VMEM((2, NC, 4, OWN, WIDE), F32),
            pltpu.VMEM((ND, OWN, WIDE), BF),
            pltpu.VMEM((ND, OWN, WIDE), BF),
            pltpu.VMEM((NC - ND, 4, 64, DW), BF),
            pltpu.VMEM((NC - ND, 4, 64, DW), BF),
            pltpu.VMEM((OWN, D), F32),
            dma((NW, 2)),
            dma((7,)),
            dma((2, NC, MSG)),
            dma((2, NC, MSG)),
            dma((2, NC, MSG)),
            dma((2, NC, MSG)),
            dma((3,)),
            dma((3,)),
        ],
        compiler_params=pltpu.CompilerParams(
            collective_id=0, has_side_effects=True, vmem_limit_bytes=VMEM_GRANT
        ),
        cost_estimate=pl.CostEstimate(
            flops=16 * 10**9, bytes_accessed=18 * 10**6, transcendentals=TOK * HID
        ),
        name="gather_compute_scatter",
    )(*arrays, fragment_rows.reshape(1, FRAG))


def copy_kernel(*refs):
    n = len(STATE)
    sems = refs[-1]
    copies = [
        pltpu.make_async_copy(refs[k], refs[n + k].at[0] if k == 0 else refs[n + k], sems.at[k])
        for k in range(n)
    ]
    for copy in copies:
        copy.start()
    for copy in copies:
        copy.wait()


def copy_out(results):
    n = len(STATE)
    return pl.pallas_call(
        copy_kernel,
        out_shape=STATE,
        in_specs=[pl.BlockSpec(memory_space=pltpu.VMEM)] * n,
        out_specs=(pl.BlockSpec(memory_space=pl.ANY),) * n,
        scratch_shapes=[pltpu.SemaphoreType.DMA((n,))],
        compiler_params=pltpu.CompilerParams(vmem_limit_bytes=8 * 2**20),
        name="copy_out",
    )(*results)


def per_device(
    tokens, w_gate, w_up, d_hidden, outer_rows, outer_momentum, adam_first, adam_second, fragment_rows
):
    return copy_out(
        exchange(
            tokens, w_gate, w_up, d_hidden, outer_rows, outer_momentum, adam_first, adam_second,
            fragment_rows,
        )
    )


def solution(mesh):
    return jax.shard_map(
        per_device,
        mesh=mesh,
        in_specs=(
            P("island", "fsdp", None),
            P("island", None, "fsdp"),
            P("island", None, "fsdp"),
            P("island", None, "fsdp"),
            P(None, None, "fsdp"),
            P(None, None, "fsdp"),
            P("island", None, None, "fsdp"),
            P("island", None, None, "fsdp"),
            P(),
        ),
        out_specs=(
            P("island", "fsdp", None),
            P("island", None, None, "fsdp"),
            P(None, None, "fsdp"),
            P(None, None, "fsdp"),
            P("island", None, None, "fsdp"),
            P("island", None, None, "fsdp"),
        ),
        check_vma=False,
    )
```

```python
import jax
import jax.numpy as jnp
from jax import lax
from jax.experimental import pallas as pl
from jax.experimental.pallas import tpu as pltpu
from jax.sharding import PartitionSpec as P

MESH = pl.DeviceIdType.MESH
BF = jnp.bfloat16
F32 = jnp.float32

D = 4096
HID = 896
W2 = 2 * HID
TOK = 512
OWN = 16
FRAG = 128
CHUNKS = ((0, 768), (768, 768), (1536, 768), (2304, 768), (3072, 512), (3584, 512))
NC = len(CHUNKS)
ND = 4
WIDE = 768
DW = 512
GATHER = (((0, 4), (0, 5)), ((0, 0), (0, 1)), ((0, 2), (0, 3)), ((1, 0), (1, 1)), ((1, 2), (1, 3)))
T = len(GATHER)
HALF = TOK // 2
FACTOR = float(D) ** (-0.5)
NW = 4
WC = D // NW
MSG = 9
VMEM_GRANT = 55 * 2**20
DECAY = 1.0 - 0.02 * 0.1


def step_kernel(
    tok_hbm, wg_hbm, wu_hbm, dh_hbm, outer_hbm, mom_hbm, first_hbm, second_hbm, row_ref,
    dtokv, fragv, outerv, momv, firstv, secondv,
    wts, toks, acc, dcat, dhid, part, oh, oht, pick, rowp, rows_all,
    sb1, rb1, sb2, rb2, quart, sbx, rbx, sbd, rbd, own_sum,
    w_sem, l_sem, ag_s, ag_r, rs_s, rs_r, is_s, is_r,
):
    isl = lax.axis_index("island")
    f = lax.axis_index("fsdp")
    x = f // 16
    z = (f // 4) % 4
    y = f % 4
    xl = isl // 2
    core = isl % 2

    def at(xx, zz, yy):
        return (isl, xx * 16 + zz * 4 + yy)

    def up(m):
        return (m + 1) % 4

    def down(m):
        return (m + 3) % 4

    def opposite(m):
        return (m + 2) % 4

    ydev = (at(x, z, up(y)), at(x, z, down(y)), at(x, z, opposite(y)))
    zdev = (at(x, up(z), y), at(x, down(z), y), at(x, opposite(z), y))
    xdev = at(1 - x, z, y)
    isl_core = xl * 2 + (1 - core)
    isl_x = (1 - xl) * 2 + core
    isl_far = 3 - isl
    cdev = (isl_core, f)
    ldev = (isl_x, f)

    def ysl(m):
        return pl.ds(pl.multiple_of(m * OWN, OWN), OWN)

    own_copy = pltpu.make_async_copy(tok_hbm.at[0], toks.at[0, z, ysl(y), :], l_sem.at[0])
    own_copy.start()
    w_copies = []
    for p in range(NW):
        rows = pl.ds(p * WC, WC)
        pair = []
        for j, src in enumerate((wg_hbm, wu_hbm)):
            copy = pltpu.make_async_copy(
                src.at[0, rows, :], wts.at[rows, pl.ds(j * HID, HID)], w_sem.at[p, j]
            )
            copy.start()
            pair.append(copy)
        w_copies.append(pair)
    dh_copies = []
    for h, plane in ((0, x), (1, 1 - x)):
        rows = pl.ds(pl.multiple_of(plane * HALF, HALF), HALF)
        copy = pltpu.make_async_copy(dh_hbm.at[0, rows, :], dhid.at[h], l_sem.at[1 + h])
        copy.start()
        dh_copies.append(copy)
    state_copies = []
    for k, (src, dst) in enumerate(
        ((outer_hbm, outerv), (mom_hbm, momv), (first_hbm, firstv), (second_hbm, secondv))
    ):
        copy = pltpu.make_async_copy(src, dst, l_sem.at[3 + k])
        copy.start()
        state_copies.append(copy)

    barrier = pltpu.get_barrier_semaphore()
    greeted = (*ydev, *zdev, xdev, cdev, ldev)
    for dev in greeted:
        pl.semaphore_signal(barrier, inc=1, device_id=dev, device_id_type=MESH)

    spread = jnp.transpose(jnp.broadcast_to(row_ref[...], (FRAG, FRAG)))

    def hot(p, _):
        lo = pl.multiple_of(p * 128, 128)
        down_rows = lax.broadcasted_iota(jnp.int32, (128, FRAG), 0) + lo
        oh[pl.ds(lo, 128), :] = jnp.where(down_rows == row_ref[...], 1.0, 0.0).astype(BF)
        along = lax.broadcasted_iota(jnp.int32, (FRAG, 128), 1) + lo
        oht[:, pl.ds(lo, 128)] = jnp.where(along == spread, 1.0, 0.0).astype(BF)
        return 0

    pl.semaphore_wait(barrier, len(greeted))

    started = []

    def send(src, dst, ss, rs, dev):
        copy = pltpu.make_async_remote_copy(
            src_ref=src, dst_ref=dst, send_sem=ss, recv_sem=rs, device_id=dev, device_id_type=MESH
        )
        copy.start()
        started.append(copy)

    def arrived(ref, rs, ss):
        pltpu.make_async_remote_copy(
            src_ref=ref, dst_ref=ref, send_sem=ss, recv_sem=rs, device_id=xdev, device_id_type=MESH
        ).wait_recv()

    def cols_of(c, half=None):
        lo, w = CHUNKS[c]
        if half is None:
            return pl.ds(lo, w)
        return pl.ds(lo + half * (w // 2), w // 2)

    def axes(c):
        return ((y, ydev), (z, zdev)) if c % 2 == 0 else ((z, zdev), (y, ydev))

    def own_part(h, c, m):
        if c % 2 == 0:
            return toks.at[h, z, ysl(m), cols_of(c)]
        return toks.at[h, m, ysl(y), cols_of(c)]

    def ring_part(h, c, m, half=None):
        if c % 2 == 0:
            return toks.at[h, m, :, cols_of(c, half)]
        return toks.at[h, :, ysl(m), cols_of(c, half)]

    def spread_own(h, c):
        (m, dev), _ = axes(c)
        for j in range(3):
            piece = own_part(h, c, m)
            source = tok_hbm.at[0, :, cols_of(c)] if h == 0 else piece
            send(source, piece, ag_s.at[h, c, 1 + j], ag_r.at[h, c, 1 + j], dev[j])

    def spread_end(h, c):
        (m, _), _ = axes(c)
        for j, other in enumerate((down(m), up(m), opposite(m))):
            arrived(own_part(h, c, other), ag_r.at[h, c, 1 + j], ag_s.at[h, c, 1 + j])

    def direct_send(c, k, m):
        send(
            ring_part(0, c, m), ring_part(1, c, m), ag_s.at[1, c, k], ag_r.at[1, c, k], xdev
        )

    def direct_end(c):
        _, (m, _) = axes(c)
        for k, other in enumerate((m, down(m), up(m), opposite(m))):
            arrived(ring_part(1, c, other), ag_r.at[1, c, k], ag_s.at[1, c, k])

    def ring_send(h, c):
        _, (m, dev) = axes(c)
        for j in range(3 if c >= ND else 2):
            piece = ring_part(h, c, m)
            send(piece, piece, ag_s.at[h, c, 5 + j], ag_r.at[h, c, 5 + j], dev[j])

    def ring_relay(h, c):
        if c >= ND:
            return
        _, (m, dev) = axes(c)
        for j, near in enumerate((down(m), up(m))):
            arrived(ring_part(h, c, near), ag_r.at[h, c, 5 + j], ag_s.at[h, c, 5 + j])
            piece = ring_part(h, c, near, j)
            send(piece, piece, ag_s.at[h, c, 7 + j], ag_r.at[h, c, 7 + j], dev[j])

    def ring_end(h, c):
        _, (m, _) = axes(c)
        if c >= ND:
            for j, other in enumerate((down(m), up(m), opposite(m))):
                arrived(ring_part(h, c, other), ag_r.at[h, c, 5 + j], ag_s.at[h, c, 5 + j])
                direct_send(c, 1 + j, other)
            return
        for j in range(2):
            arrived(ring_part(h, c, opposite(m), j), ag_r.at[h, c, 7 + j], ag_s.at[h, c, 7 + j])

    for pair in GATHER[:3]:
        for h, c in pair:
            spread_own(h, c)
    for c in range(ND):
        send(
            tok_hbm.at[0, :, cols_of(c)], toks.at[1, z, ysl(y), cols_of(c)],
            ag_s.at[1, c, 0], ag_r.at[1, c, 0], xdev,
        )
    lax.fori_loop(0, D // 128, hot, 0)
    own_copy.wait()

    def spread_partner():
        for c in range(ND):
            arrived(toks.at[1, z, ysl(y), cols_of(c)], ag_r.at[1, c, 0], ag_s.at[1, c, 0])
            spread_own(1, c)

    def pick_rows(p):
        for copy in w_copies[p]:
            copy.wait()
        value = jnp.dot(
            oht[:, p * WC:(p + 1) * WC], wts[p * WC:(p + 1) * WC, :], preferred_element_type=F32
        )
        rowp[...] = value if p == 0 else value + rowp[...]

    def pick_all(lo, hi):
        for p in range(lo, hi):
            pick_rows(p)

    def share_rows():
        rows_all[isl] = rowp[...].astype(BF)
        send(rows_all.at[isl], rows_all.at[isl], is_s.at[0], is_r.at[0], cdev)
        send(rows_all.at[isl], rows_all.at[isl], is_s.at[1], is_r.at[1], ldev)

    begun = set()

    def forward(h, c):
        start = h not in begun
        begun.add(h)
        lo, w = CHUNKS[c]
        hi = lo + w
        lhs = toks[h, :, :, lo:hi].reshape(HALF, w)
        value = jnp.dot(lhs, wts[lo:hi, :], preferred_element_type=F32)
        acc[h] = value if start else value + acc[h]
        value = jnp.dot(lhs, oh[lo:hi, :], preferred_element_type=F32)
        pick[h] = value if start else value + pick[h]

    def gated(h):
        dh_copies[h].wait()

        def body(r, _):
            rr = pl.ds(pl.multiple_of(r * 16, 16), 16)
            gate = acc[h, rr, 0:HID] * FACTOR
            upv = acc[h, rr, HID:W2] * FACTOR
            g = dhid[h, rr, :].astype(F32)
            s = jax.nn.sigmoid(gate)
            dcat[h, rr, 0:HID] = (g * upv * (s * (1.0 + gate * (1.0 - s)))).astype(BF)
            dcat[h, rr, HID:W2] = (g * (gate * s)).astype(BF)
            return 0

        lax.fori_loop(0, HALF // 16, body, 0)

    def backward(h, c):
        lo, w = CHUNKS[c]
        hi = lo + w
        value = lax.dot_general(
            dcat[h], wts[lo:hi, :], (((1,), (1,)), ((), ())), preferred_element_type=F32
        )
        if h == 1 and c >= ND:
            sbd[c - ND] = value.reshape(4, 64, w).astype(BF)
            send(sbd.at[c - ND], rbd.at[c - ND], rs_s.at[h, c, 8], rs_r.at[h, c, 8], xdev)
            return
        part[h, :, :, lo:hi] = value.reshape(4, 64, w)

    def join(c):
        arrived(rbd.at[c - ND], rs_r.at[1, c, 8], rs_s.at[1, c, 8])
        part[0, :, :, cols_of(c)] = part[0, :, :, cols_of(c)] + rbd[c - ND].astype(F32)

    def scatter_axes(c):
        return ((z, zdev), (y, ydev)) if c % 2 == 0 else ((y, ydev), (z, zdev))

    def block1(h, c, m, half=None):
        if c % 2 == 0:
            return part[h, m, :, cols_of(c, half)]
        w = CHUNKS[c][1]
        return part[h, :, ysl(m), cols_of(c, half)].reshape(64, w if half is None else w // 2)

    def wide(c):
        return pl.ds(0, CHUNKS[c][1])

    def halves(c, j):
        w = CHUNKS[c][1] // 2
        return pl.ds(j * w, w)

    def far_out(h, c):
        (m, dev), _ = scatter_axes(c)
        if c >= ND:
            w = wide(c)
            for j, other in enumerate((up(m), down(m), opposite(m))):
                sb1[h, c, j, :, w] = block1(h, c, other).astype(BF)
                send(
                    sb1.at[h, c, j, :, w], rb1.at[h, c, j, :, w],
                    rs_s.at[h, c, j], rs_r.at[h, c, j], dev[j],
                )
            return
        sb1[h, c, 0, :, wide(c)] = block1(h, c, opposite(m)).astype(BF)
        for j in range(2):
            hs = halves(c, j)
            send(
                sb1.at[h, c, 0, :, hs], rb1.at[h, c, 0, :, hs],
                rs_s.at[h, c, j], rs_r.at[h, c, j], dev[j],
            )

    def near_out(h, c):
        (m, dev), _ = scatter_axes(c)
        for j, near in enumerate((up(m), down(m))):
            hs = halves(c, j)
            ot = halves(c, 1 - j)
            sb1[h, c, 1 + j, :, ot] = block1(h, c, near, 1 - j).astype(BF)
            arrived(rb1.at[h, c, 0, :, hs], rs_r.at[h, c, j], rs_s.at[h, c, j])
            sb1[h, c, 1 + j, :, hs] = (
                block1(h, c, near, j) + rb1[h, c, 0, :, hs].astype(F32)
            ).astype(BF)
            send(
                sb1.at[h, c, 1 + j, :, wide(c)], rb1.at[h, c, 1 + j, :, wide(c)],
                rs_s.at[h, c, 2 + j], rs_r.at[h, c, 2 + j], dev[j],
            )

    def ring_total(h, c):
        w = wide(c)
        (m, _), (m2, dev2) = scatter_axes(c)
        for j in range(3 if c >= ND else 2):
            k = j if c >= ND else 1 + j
            e = j if c >= ND else 2 + j
            arrived(rb1.at[h, c, k, :, w], rs_r.at[h, c, e], rs_s.at[h, c, e])
        value = rb1[h, c, 1, :, w].astype(F32) + rb1[h, c, 2, :, w].astype(F32)
        if c >= ND:
            value = value + rb1[h, c, 0, :, w].astype(F32)
        value = block1(h, c, m) + value
        quart[h, c, :, :, w] = value.reshape(4, OWN, CHUNKS[c][1])
        for j, other in enumerate((up(m2), down(m2), opposite(m2))):
            sb2[h, c, j, :, w] = quart[h, c, other, :, w].astype(BF)
            send(
                sb2.at[h, c, j, :, w], rb2.at[h, c, j, :, w],
                rs_s.at[h, c, 4 + j], rs_r.at[h, c, 4 + j], dev2[j],
            )

    def plane_total(h, c):
        w = wide(c)
        _, (m2, _) = scatter_axes(c)
        for j in range(3):
            arrived(rb2.at[h, c, j, :, w], rs_r.at[h, c, 4 + j], rs_s.at[h, c, 4 + j])
        value = quart[h, c, m2, :, w] + (
            (rb2[h, c, 0, :, w].astype(F32) + rb2[h, c, 1, :, w].astype(F32))
            + rb2[h, c, 2, :, w].astype(F32)
        )
        if h == 1:
            sbx[c, :, w] = value.astype(BF)
            send(sbx.at[c, :, w], rbx.at[c, :, w], rs_s.at[h, c, 8], rs_r.at[h, c, 8], xdev)
        elif c < ND:
            own_sum[:, cols_of(c)] = value
        else:
            dtokv[:, cols_of(c)] = (value * FACTOR).astype(BF)

    def finish(c):
        arrived(rbx.at[c, :, wide(c)], rs_r.at[1, c, 8], rs_s.at[1, c, 8])
        value = own_sum[:, cols_of(c)] + rbx[c, :, wide(c)].astype(F32)
        dtokv[:, cols_of(c)] = (value * FACTOR).astype(BF)

    def gradient():
        pk = jnp.transpose(pick[...].reshape(TOK, FRAG)).astype(BF)
        acc[0, 0:FRAG, :] = (
            jnp.dot(pk, dcat[...].reshape(TOK, W2), preferred_element_type=F32) * FACTOR
        )

    def pass_rows():
        arrived(rows_all.at[isl_x], is_r.at[1], is_s.at[1])
        send(rows_all.at[isl_x], rows_all.at[isl_x], is_s.at[2], is_r.at[2], cdev)

    def optimize():
        arrived(rows_all.at[isl_core], is_r.at[0], is_s.at[0])
        arrived(rows_all.at[isl_far], is_r.at[2], is_s.at[2])
        for copy in state_copies:
            copy.wait()

        def body(i, _):
            rr = pl.ds(pl.multiple_of(i * 16, 16), 16)
            for j in range(2):
                cols = pl.ds(j * HID, HID)
                rsum = rows_all[0, rr, cols].astype(F32)
                for k in range(1, 4):
                    rsum = rsum + rows_all[k, rr, cols].astype(F32)
                outer = outerv[j, rr]
                g = acc[0, rr, cols]
                mean_delta = outer - rsum * 0.25
                mom = 0.9 * momv[j, rr] + mean_delta
                outer = outer - 0.7 * (mean_delta + 0.9 * mom)
                first = 0.9 * firstv[0, j, rr] + 0.1 * g
                second = 0.95 * secondv[0, j, rr] + 0.05 * (g * g)
                momv[j, rr] = mom
                outerv[j, rr] = outer
                firstv[0, j, rr] = first
                secondv[0, j, rr] = second
                fragv[0, j, rr] = (
                    outer * DECAY - 0.02 * first / (jnp.sqrt(second) + 1e-08)
                ).astype(BF)
            return 0

        lax.fori_loop(0, FRAG // 16, body, 0)

    def each(work, items):
        for item in items:
            work(*item)

    o_direct, o_one, o_two, p_one, p_two = GATHER
    direct = range(ND, NC)

    def ring_start(items):
        for item in items:
            spread_end(*item)
            ring_send(*item)

    def multiply(items):
        for item in items:
            ring_end(*item)
            forward(*item)

    ring_start(o_direct)
    for c in direct:
        direct_send(c, 0, axes(c)[1][0])
    pick_all(0, 1)
    ring_start(o_one)
    spread_partner()
    ring_start(o_two)
    pick_all(1, 2)
    each(ring_end, o_direct)
    pick_all(2, 4)
    share_rows()
    each(ring_relay, o_one)
    each(forward, o_direct)
    ring_start(p_one)
    each(ring_relay, o_two)
    ring_start(p_two)
    multiply(o_one)
    each(ring_relay, p_one)
    multiply(o_two)
    gated(0)

    def multiply_back(items):
        for item in items:
            backward(*item)
            far_out(*item)

    each(ring_relay, p_two)
    multiply_back(o_one)
    multiply(p_one)
    multiply_back(o_two)
    each(near_out, o_one)
    multiply(p_two)
    for c in direct:
        direct_end(c)
        forward(1, c)
    gated(1)
    each(near_out, o_two)

    for c in direct:
        backward(1, c)
    multiply_back(p_one)
    each(ring_total, o_one)
    multiply_back(p_two)
    each(ring_total, o_two)
    each(near_out, p_one)
    pass_rows()
    each(plane_total, o_one)
    each(backward, o_direct)
    each(near_out, p_two)
    join(ND)
    far_out(0, ND)
    each(plane_total, o_two)
    each(ring_total, p_one)
    gradient()
    each(ring_total, p_two)
    join(ND + 1)
    far_out(0, ND + 1)
    each(plane_total, p_one)
    optimize()
    ring_total(0, ND)
    each(plane_total, p_two)
    ring_total(0, ND + 1)
    plane_total(0, ND)
    for c in range(ND):
        finish(c)
    plane_total(0, ND + 1)

    for copy in started:
        copy.wait_send()


STATE = (
    jax.ShapeDtypeStruct((1, OWN, D), BF),
    jax.ShapeDtypeStruct((1, 2, FRAG, HID), BF),
    jax.ShapeDtypeStruct((2, FRAG, HID), F32),
    jax.ShapeDtypeStruct((2, FRAG, HID), F32),
    jax.ShapeDtypeStruct((1, 2, FRAG, HID), F32),
    jax.ShapeDtypeStruct((1, 2, FRAG, HID), F32),
)


def exchange(*args):
    any_spec = pl.BlockSpec(memory_space=pl.ANY)
    vmem = pl.BlockSpec(memory_space=pltpu.VMEM)
    dma = pltpu.SemaphoreType.DMA
    *arrays, fragment_rows = args
    return pl.pallas_call(
        step_kernel,
        out_shape=tuple(pltpu.VMEM(s.shape, s.dtype) for s in (jax.ShapeDtypeStruct((OWN, D), BF),) + STATE[1:]),
        in_specs=[any_spec] * 8 + [vmem],
        out_specs=(vmem,) * 6,
        scratch_shapes=[
            pltpu.VMEM((D, W2), BF),
            pltpu.VMEM((2, 4, 64, D), BF),
            pltpu.VMEM((2, HALF, W2), F32),
            pltpu.VMEM((2, HALF, W2), BF),
            pltpu.VMEM((2, HALF, HID), BF),
            pltpu.VMEM((2, 4, 64, D), F32),
            pltpu.VMEM((D, FRAG), BF),
            pltpu.VMEM((FRAG, D), BF),
            pltpu.VMEM((2, HALF, FRAG), F32),
            pltpu.VMEM((FRAG, W2), F32),
            pltpu.VMEM((4, FRAG, W2), BF),
            pltpu.VMEM((2, NC, 3, 64, WIDE), BF),
            pltpu.VMEM((2, NC, 3, 64, WIDE), BF),
            pltpu.VMEM((2, NC, 3, OWN, WIDE), BF),
            pltpu.VMEM((2, NC, 3, OWN, WIDE), BF),
            pltpu.VMEM((2, NC, 4, OWN, WIDE), F32),
            pltpu.VMEM((ND, OWN, WIDE), BF),
            pltpu.VMEM((ND, OWN, WIDE), BF),
            pltpu.VMEM((NC - ND, 4, 64, DW), BF),
            pltpu.VMEM((NC - ND, 4, 64, DW), BF),
            pltpu.VMEM((OWN, D), F32),
            dma((NW, 2)),
            dma((7,)),
            dma((2, NC, MSG)),
            dma((2, NC, MSG)),
            dma((2, NC, MSG)),
            dma((2, NC, MSG)),
            dma((3,)),
            dma((3,)),
        ],
        compiler_params=pltpu.CompilerParams(
            collective_id=0, has_side_effects=True, vmem_limit_bytes=VMEM_GRANT
        ),
        cost_estimate=pl.CostEstimate(
            flops=16 * 10**9, bytes_accessed=18 * 10**6, transcendentals=TOK * HID
        ),
        name="gather_compute_scatter",
    )(*arrays, fragment_rows.reshape(1, FRAG))


def copy_kernel(*refs):
    n = len(STATE)
    sems = refs[-1]
    copies = [
        pltpu.make_async_copy(refs[k], refs[n + k].at[0] if k == 0 else refs[n + k], sems.at[k])
        for k in range(n)
    ]
    for copy in copies:
        copy.start()
    for copy in copies:
        copy.wait()


def copy_out(results):
    n = len(STATE)
    return pl.pallas_call(
        copy_kernel,
        out_shape=STATE,
        in_specs=[pl.BlockSpec(memory_space=pltpu.VMEM)] * n,
        out_specs=(pl.BlockSpec(memory_space=pl.ANY),) * n,
        scratch_shapes=[pltpu.SemaphoreType.DMA((n,))],
        compiler_params=pltpu.CompilerParams(vmem_limit_bytes=8 * 2**20),
        name="copy_out",
    )(*results)


def per_device(
    tokens, w_gate, w_up, d_hidden, outer_rows, outer_momentum, adam_first, adam_second, fragment_rows
):
    return copy_out(
        exchange(
            tokens, w_gate, w_up, d_hidden, outer_rows, outer_momentum, adam_first, adam_second,
            fragment_rows,
        )
    )


def solution(mesh):
    return jax.shard_map(
        per_device,
        mesh=mesh,
        in_specs=(
            P("island", "fsdp", None),
            P("island", None, "fsdp"),
            P("island", None, "fsdp"),
            P("island", None, "fsdp"),
            P(None, None, "fsdp"),
            P(None, None, "fsdp"),
            P("island", None, None, "fsdp"),
            P("island", None, None, "fsdp"),
            P(),
        ),
        out_specs=(
            P("island", "fsdp", None),
            P("island", None, None, "fsdp"),
            P(None, None, "fsdp"),
            P(None, None, "fsdp"),
            P("island", None, None, "fsdp"),
            P("island", None, None, "fsdp"),
        ),
        check_vma=False,
    )
```

```python
import jax
import jax.numpy as jnp
from jax import lax
from jax.experimental import pallas as pl
from jax.experimental.pallas import tpu as pltpu
from jax.sharding import PartitionSpec as P

MESH = pl.DeviceIdType.MESH
BF = jnp.bfloat16
F32 = jnp.float32

D = 4096
HID = 896
W2 = 2 * HID
TOK = 512
OWN = 16
FRAG = 128
CHUNKS = ((0, 768), (768, 768), (1536, 768), (2304, 768), (3072, 512), (3584, 512))
NC = len(CHUNKS)
ND = 4
WIDE = 768
DW = 512
GATHER = (((0, 4), (0, 5)), ((0, 0), (0, 1)), ((0, 2), (0, 3)), ((1, 0), (1, 1)), ((1, 2), (1, 3)))
T = len(GATHER)
HALF = TOK // 2
FACTOR = float(D) ** (-0.5)
NW = 4
WC = D // NW
MSG = 9
VMEM_GRANT = 55 * 2**20
DECAY = 1.0 - 0.02 * 0.1


def step_kernel(
    tok_hbm, wg_hbm, wu_hbm, dh_hbm, outer_hbm, mom_hbm, first_hbm, second_hbm, row_ref,
    dtokv, fragv, outerv, momv, firstv, secondv,
    wts, toks, acc, dcat, dhid, part, oh, oht, pick, rowp, rows_all,
    sb1, rb1, sb2, rb2, quart, sbx, rbx, sbd, rbd, own_sum,
    w_sem, l_sem, ag_s, ag_r, rs_s, rs_r, is_s, is_r,
):
    isl = lax.axis_index("island")
    f = lax.axis_index("fsdp")
    x = f // 16
    z = (f // 4) % 4
    y = f % 4
    xl = isl // 2
    core = isl % 2

    def at(xx, zz, yy):
        return (isl, xx * 16 + zz * 4 + yy)

    def up(m):
        return (m + 1) % 4

    def down(m):
        return (m + 3) % 4

    def opposite(m):
        return (m + 2) % 4

    ydev = (at(x, z, up(y)), at(x, z, down(y)), at(x, z, opposite(y)))
    zdev = (at(x, up(z), y), at(x, down(z), y), at(x, opposite(z), y))
    xdev = at(1 - x, z, y)
    isl_core = xl * 2 + (1 - core)
    isl_x = (1 - xl) * 2 + core
    isl_far = 3 - isl
    cdev = (isl_core, f)
    ldev = (isl_x, f)

    def ysl(m):
        return pl.ds(pl.multiple_of(m * OWN, OWN), OWN)

    own_copy = pltpu.make_async_copy(tok_hbm.at[0], toks.at[0, z, ysl(y), :], l_sem.at[0])
    own_copy.start()
    w_copies = []
    for p in range(NW):
        rows = pl.ds(p * WC, WC)
        pair = []
        for j, src in enumerate((wg_hbm, wu_hbm)):
            copy = pltpu.make_async_copy(
                src.at[0, rows, :], wts.at[rows, pl.ds(j * HID, HID)], w_sem.at[p, j]
            )
            copy.start()
            pair.append(copy)
        w_copies.append(pair)
    dh_copies = []
    for h, plane in ((0, x), (1, 1 - x)):
        rows = pl.ds(pl.multiple_of(plane * HALF, HALF), HALF)
        copy = pltpu.make_async_copy(dh_hbm.at[0, rows, :], dhid.at[h], l_sem.at[1 + h])
        copy.start()
        dh_copies.append(copy)
    state_copies = []
    for k, (src, dst) in enumerate(
        ((outer_hbm, outerv), (mom_hbm, momv), (first_hbm, firstv), (second_hbm, secondv))
    ):
        copy = pltpu.make_async_copy(src, dst, l_sem.at[3 + k])
        copy.start()
        state_copies.append(copy)

    barrier = pltpu.get_barrier_semaphore()
    greeted = (*ydev, *zdev, xdev, cdev, ldev)
    for dev in greeted:
        pl.semaphore_signal(barrier, inc=1, device_id=dev, device_id_type=MESH)

    spread = jnp.transpose(jnp.broadcast_to(row_ref[...], (FRAG, FRAG)))

    def hot(p, _):
        lo = pl.multiple_of(p * 128, 128)
        down_rows = lax.broadcasted_iota(jnp.int32, (128, FRAG), 0) + lo
        oh[pl.ds(lo, 128), :] = jnp.where(down_rows == row_ref[...], 1.0, 0.0).astype(BF)
        along = lax.broadcasted_iota(jnp.int32, (FRAG, 128), 1) + lo
        oht[:, pl.ds(lo, 128)] = jnp.where(along == spread, 1.0, 0.0).astype(BF)
        return 0

    pl.semaphore_wait(barrier, len(greeted))

    started = []

    def send(src, dst, ss, rs, dev):
        copy = pltpu.make_async_remote_copy(
            src_ref=src, dst_ref=dst, send_sem=ss, recv_sem=rs, device_id=dev, device_id_type=MESH
        )
        copy.start()
        started.append(copy)

    def arrived(ref, rs, ss):
        pltpu.make_async_remote_copy(
            src_ref=ref, dst_ref=ref, send_sem=ss, recv_sem=rs, device_id=xdev, device_id_type=MESH
        ).wait_recv()

    def cols_of(c, half=None):
        lo, w = CHUNKS[c]
        if half is None:
            return pl.ds(lo, w)
        return pl.ds(lo + half * (w // 2), w // 2)

    def axes(c):
        return ((y, ydev), (z, zdev)) if c % 2 == 0 else ((z, zdev), (y, ydev))

    def own_part(h, c, m):
        if c % 2 == 0:
            return toks.at[h, z, ysl(m), cols_of(c)]
        return toks.at[h, m, ysl(y), cols_of(c)]

    def ring_part(h, c, m, half=None):
        if c % 2 == 0:
            return toks.at[h, m, :, cols_of(c, half)]
        return toks.at[h, :, ysl(m), cols_of(c, half)]

    def spread_own(h, c):
        (m, dev), _ = axes(c)
        for j in range(3):
            piece = own_part(h, c, m)
            source = tok_hbm.at[0, :, cols_of(c)] if h == 0 else piece
            send(source, piece, ag_s.at[h, c, 1 + j], ag_r.at[h, c, 1 + j], dev[j])

    def spread_end(h, c):
        (m, _), _ = axes(c)
        for j, other in enumerate((down(m), up(m), opposite(m))):
            arrived(own_part(h, c, other), ag_r.at[h, c, 1 + j], ag_s.at[h, c, 1 + j])

    def direct_send(c, k, m):
        send(
            ring_part(0, c, m), ring_part(1, c, m), ag_s.at[1, c, k], ag_r.at[1, c, k], xdev
        )

    def direct_end(c):
        _, (m, _) = axes(c)
        for k, other in enumerate((m, down(m), up(m), opposite(m))):
            arrived(ring_part(1, c, other), ag_r.at[1, c, k], ag_s.at[1, c, k])

    def ring_send(h, c):
        _, (m, dev) = axes(c)
        for j in range(3 if c >= ND else 2):
            piece = ring_part(h, c, m)
            send(piece, piece, ag_s.at[h, c, 5 + j], ag_r.at[h, c, 5 + j], dev[j])

    def ring_relay(h, c):
        if c >= ND:
            return
        _, (m, dev) = axes(c)
        for j, near in enumerate((down(m), up(m))):
            arrived(ring_part(h, c, near), ag_r.at[h, c, 5 + j], ag_s.at[h, c, 5 + j])
            piece = ring_part(h, c, near, j)
            send(piece, piece, ag_s.at[h, c, 7 + j], ag_r.at[h, c, 7 + j], dev[j])

    def ring_end(h, c):
        _, (m, _) = axes(c)
        if c >= ND:
            for j, other in enumerate((down(m), up(m), opposite(m))):
                arrived(ring_part(h, c, other), ag_r.at[h, c, 5 + j], ag_s.at[h, c, 5 + j])
                direct_send(c, 1 + j, other)
            return
        for j in range(2):
            arrived(ring_part(h, c, opposite(m), j), ag_r.at[h, c, 7 + j], ag_s.at[h, c, 7 + j])

    for pair in GATHER[:3]:
        for h, c in pair:
            spread_own(h, c)
    for c in range(ND):
        send(
            tok_hbm.at[0, :, cols_of(c)], toks.at[1, z, ysl(y), cols_of(c)],
            ag_s.at[1, c, 0], ag_r.at[1, c, 0], xdev,
        )
    lax.fori_loop(0, D // 128, hot, 0)
    own_copy.wait()

    def spread_partner():
        for c in range(ND):
            arrived(toks.at[1, z, ysl(y), cols_of(c)], ag_r.at[1, c, 0], ag_s.at[1, c, 0])
            spread_own(1, c)

    def pick_rows(p):
        for copy in w_copies[p]:
            copy.wait()
        value = jnp.dot(
            oht[:, p * WC:(p + 1) * WC], wts[p * WC:(p + 1) * WC, :], preferred_element_type=F32
        )
        rowp[...] = value if p == 0 else value + rowp[...]

    def pick_all(lo, hi):
        for p in range(lo, hi):
            pick_rows(p)

    def share_rows():
        rows_all[isl] = rowp[...].astype(BF)
        send(rows_all.at[isl], rows_all.at[isl], is_s.at[0], is_r.at[0], cdev)
        send(rows_all.at[isl], rows_all.at[isl], is_s.at[1], is_r.at[1], ldev)

    begun = set()

    def forward(h, c):
        start = h not in begun
        begun.add(h)
        lo, w = CHUNKS[c]
        hi = lo + w
        lhs = toks[h, :, :, lo:hi].reshape(HALF, w)
        value = jnp.dot(lhs, wts[lo:hi, :], preferred_element_type=F32)
        acc[h] = value if start else value + acc[h]

    def pick_columns(h):
        pick[h] = jnp.dot(toks[h].reshape(HALF, D), oh[...], preferred_element_type=F32)

    def gated(h):
        dh_copies[h].wait()

        def body(r, _):
            rr = pl.ds(pl.multiple_of(r * 16, 16), 16)
            gate = acc[h, rr, 0:HID] * FACTOR
            upv = acc[h, rr, HID:W2] * FACTOR
            g = dhid[h, rr, :].astype(F32)
            s = jax.nn.sigmoid(gate)
            dcat[h, rr, 0:HID] = (g * upv * (s * (1.0 + gate * (1.0 - s)))).astype(BF)
            dcat[h, rr, HID:W2] = (g * (gate * s)).astype(BF)
            return 0

        lax.fori_loop(0, HALF // 16, body, 0)

    def backward(h, c):
        lo, w = CHUNKS[c]
        hi = lo + w
        value = lax.dot_general(
            dcat[h], wts[lo:hi, :], (((1,), (1,)), ((), ())), preferred_element_type=F32
        )
        if h == 1 and c >= ND:
            sbd[c - ND] = value.reshape(4, 64, w).astype(BF)
            send(sbd.at[c - ND], rbd.at[c - ND], rs_s.at[h, c, 8], rs_r.at[h, c, 8], xdev)
            return
        part[h, :, :, lo:hi] = value.reshape(4, 64, w)

    def join(c):
        arrived(rbd.at[c - ND], rs_r.at[1, c, 8], rs_s.at[1, c, 8])
        part[0, :, :, cols_of(c)] = part[0, :, :, cols_of(c)] + rbd[c - ND].astype(F32)

    def scatter_axes(c):
        return ((z, zdev), (y, ydev)) if c % 2 == 0 else ((y, ydev), (z, zdev))

    def block1(h, c, m, half=None):
        if c % 2 == 0:
            return part[h, m, :, cols_of(c, half)]
        w = CHUNKS[c][1]
        return part[h, :, ysl(m), cols_of(c, half)].reshape(64, w if half is None else w // 2)

    def wide(c):
        return pl.ds(0, CHUNKS[c][1])

    def halves(c, j):
        w = CHUNKS[c][1] // 2
        return pl.ds(j * w, w)

    def far_out(h, c):
        (m, dev), _ = scatter_axes(c)
        if c >= ND:
            w = wide(c)
            for j, other in enumerate((up(m), down(m), opposite(m))):
                sb1[h, c, j, :, w] = block1(h, c, other).astype(BF)
                send(
                    sb1.at[h, c, j, :, w], rb1.at[h, c, j, :, w],
                    rs_s.at[h, c, j], rs_r.at[h, c, j], dev[j],
                )
            return
        sb1[h, c, 0, :, wide(c)] = block1(h, c, opposite(m)).astype(BF)
        for j in range(2):
            hs = halves(c, j)
            send(
                sb1.at[h, c, 0, :, hs], rb1.at[h, c, 0, :, hs],
                rs_s.at[h, c, j], rs_r.at[h, c, j], dev[j],
            )

    def near_out(h, c):
        (m, dev), _ = scatter_axes(c)
        for j, near in enumerate((up(m), down(m))):
            hs = halves(c, j)
            ot = halves(c, 1 - j)
            sb1[h, c, 1 + j, :, ot] = block1(h, c, near, 1 - j).astype(BF)
            arrived(rb1.at[h, c, 0, :, hs], rs_r.at[h, c, j], rs_s.at[h, c, j])
            sb1[h, c, 1 + j, :, hs] = (
                block1(h, c, near, j) + rb1[h, c, 0, :, hs].astype(F32)
            ).astype(BF)
            send(
                sb1.at[h, c, 1 + j, :, wide(c)], rb1.at[h, c, 1 + j, :, wide(c)],
                rs_s.at[h, c, 2 + j], rs_r.at[h, c, 2 + j], dev[j],
            )

    def ring_total(h, c):
        w = wide(c)
        (m, _), (m2, dev2) = scatter_axes(c)
        for j in range(3 if c >= ND else 2):
            k = j if c >= ND else 1 + j
            e = j if c >= ND else 2 + j
            arrived(rb1.at[h, c, k, :, w], rs_r.at[h, c, e], rs_s.at[h, c, e])
        value = rb1[h, c, 1, :, w].astype(F32) + rb1[h, c, 2, :, w].astype(F32)
        if c >= ND:
            value = value + rb1[h, c, 0, :, w].astype(F32)
        value = block1(h, c, m) + value
        quart[h, c, :, :, w] = value.reshape(4, OWN, CHUNKS[c][1])
        for j, other in enumerate((up(m2), down(m2), opposite(m2))):
            sb2[h, c, j, :, w] = quart[h, c, other, :, w].astype(BF)
            send(
                sb2.at[h, c, j, :, w], rb2.at[h, c, j, :, w],
                rs_s.at[h, c, 4 + j], rs_r.at[h, c, 4 + j], dev2[j],
            )

    def plane_total(h, c):
        w = wide(c)
        _, (m2, _) = scatter_axes(c)
        for j in range(3):
            arrived(rb2.at[h, c, j, :, w], rs_r.at[h, c, 4 + j], rs_s.at[h, c, 4 + j])
        value = quart[h, c, m2, :, w] + (
            (rb2[h, c, 0, :, w].astype(F32) + rb2[h, c, 1, :, w].astype(F32))
            + rb2[h, c, 2, :, w].astype(F32)
        )
        if h == 1:
            sbx[c, :, w] = value.astype(BF)
            send(sbx.at[c, :, w], rbx.at[c, :, w], rs_s.at[h, c, 8], rs_r.at[h, c, 8], xdev)
        elif c < ND:
            own_sum[:, cols_of(c)] = value
        else:
            dtokv[:, cols_of(c)] = (value * FACTOR).astype(BF)

    def finish(c):
        arrived(rbx.at[c, :, wide(c)], rs_r.at[1, c, 8], rs_s.at[1, c, 8])
        value = own_sum[:, cols_of(c)] + rbx[c, :, wide(c)].astype(F32)
        dtokv[:, cols_of(c)] = (value * FACTOR).astype(BF)

    def gradient():
        pk = jnp.transpose(pick[...].reshape(TOK, FRAG)).astype(BF)
        acc[0, 0:FRAG, :] = (
            jnp.dot(pk, dcat[...].reshape(TOK, W2), preferred_element_type=F32) * FACTOR
        )

    def pass_rows():
        arrived(rows_all.at[isl_x], is_r.at[1], is_s.at[1])
        send(rows_all.at[isl_x], rows_all.at[isl_x], is_s.at[2], is_r.at[2], cdev)

    def optimize():
        arrived(rows_all.at[isl_core], is_r.at[0], is_s.at[0])
        arrived(rows_all.at[isl_far], is_r.at[2], is_s.at[2])
        for copy in state_copies:
            copy.wait()

        def body(i, _):
            rr = pl.ds(pl.multiple_of(i * 16, 16), 16)
            for j in range(2):
                cols = pl.ds(j * HID, HID)
                rsum = rows_all[0, rr, cols].astype(F32)
                for k in range(1, 4):
                    rsum = rsum + rows_all[k, rr, cols].astype(F32)
                outer = outerv[j, rr]
                g = acc[0, rr, cols]
                mean_delta = outer - rsum * 0.25
                mom = 0.9 * momv[j, rr] + mean_delta
                outer = outer - 0.7 * (mean_delta + 0.9 * mom)
                first = 0.9 * firstv[0, j, rr] + 0.1 * g
                second = 0.95 * secondv[0, j, rr] + 0.05 * (g * g)
                momv[j, rr] = mom
                outerv[j, rr] = outer
                firstv[0, j, rr] = first
                secondv[0, j, rr] = second
                fragv[0, j, rr] = (
                    outer * DECAY - 0.02 * first / (jnp.sqrt(second) + 1e-08)
                ).astype(BF)
            return 0

        lax.fori_loop(0, FRAG // 16, body, 0)

    def each(work, items):
        for item in items:
            work(*item)

    o_direct, o_one, o_two, p_one, p_two = GATHER
    direct = range(ND, NC)

    def ring_start(items):
        for item in items:
            spread_end(*item)
            ring_send(*item)

    def multiply(items):
        for item in items:
            ring_end(*item)
            forward(*item)

    ring_start(o_direct)
    for c in direct:
        direct_send(c, 0, axes(c)[1][0])
    pick_all(0, 1)
    ring_start(o_one)
    spread_partner()
    ring_start(o_two)
    pick_all(1, 2)
    each(ring_end, o_direct)
    pick_all(2, 4)
    share_rows()
    each(ring_relay, o_one)
    each(forward, o_direct)
    ring_start(p_one)
    each(ring_relay, o_two)
    ring_start(p_two)
    multiply(o_one)
    each(ring_relay, p_one)
    multiply(o_two)
    gated(0)

    def multiply_back(items):
        for item in items:
            backward(*item)
            far_out(*item)

    each(ring_relay, p_two)
    multiply_back(o_one)
    multiply(p_one)
    multiply_back(o_two)
    each(near_out, o_one)
    multiply(p_two)
    for c in direct:
        direct_end(c)
        forward(1, c)
    gated(1)
    each(near_out, o_two)

    for c in direct:
        backward(1, c)
    multiply_back(p_one)
    each(ring_total, o_one)
    multiply_back(p_two)
    each(ring_total, o_two)
    each(near_out, p_one)
    pass_rows()
    each(plane_total, o_one)
    pick_columns(0)
    pick_columns(1)
    each(backward, o_direct)
    each(near_out, p_two)
    join(ND)
    far_out(0, ND)
    each(plane_total, o_two)
    each(ring_total, p_one)
    gradient()
    each(ring_total, p_two)
    join(ND + 1)
    far_out(0, ND + 1)
    each(plane_total, p_one)
    optimize()
    ring_total(0, ND)
    each(plane_total, p_two)
    ring_total(0, ND + 1)
    plane_total(0, ND)
    for c in range(ND):
        finish(c)
    plane_total(0, ND + 1)

    for copy in started:
        copy.wait_send()


STATE = (
    jax.ShapeDtypeStruct((1, OWN, D), BF),
    jax.ShapeDtypeStruct((1, 2, FRAG, HID), BF),
    jax.ShapeDtypeStruct((2, FRAG, HID), F32),
    jax.ShapeDtypeStruct((2, FRAG, HID), F32),
    jax.ShapeDtypeStruct((1, 2, FRAG, HID), F32),
    jax.ShapeDtypeStruct((1, 2, FRAG, HID), F32),
)


def exchange(*args):
    any_spec = pl.BlockSpec(memory_space=pl.ANY)
    vmem = pl.BlockSpec(memory_space=pltpu.VMEM)
    dma = pltpu.SemaphoreType.DMA
    *arrays, fragment_rows = args
    return pl.pallas_call(
        step_kernel,
        out_shape=tuple(pltpu.VMEM(s.shape, s.dtype) for s in (jax.ShapeDtypeStruct((OWN, D), BF),) + STATE[1:]),
        in_specs=[any_spec] * 8 + [vmem],
        out_specs=(vmem,) * 6,
        scratch_shapes=[
            pltpu.VMEM((D, W2), BF),
            pltpu.VMEM((2, 4, 64, D), BF),
            pltpu.VMEM((2, HALF, W2), F32),
            pltpu.VMEM((2, HALF, W2), BF),
            pltpu.VMEM((2, HALF, HID), BF),
            pltpu.VMEM((2, 4, 64, D), F32),
            pltpu.VMEM((D, FRAG), BF),
            pltpu.VMEM((FRAG, D), BF),
            pltpu.VMEM((2, HALF, FRAG), F32),
            pltpu.VMEM((FRAG, W2), F32),
            pltpu.VMEM((4, FRAG, W2), BF),
            pltpu.VMEM((2, NC, 3, 64, WIDE), BF),
            pltpu.VMEM((2, NC, 3, 64, WIDE), BF),
            pltpu.VMEM((2, NC, 3, OWN, WIDE), BF),
            pltpu.VMEM((2, NC, 3, OWN, WIDE), BF),
            pltpu.VMEM((2, NC, 4, OWN, WIDE), F32),
            pltpu.VMEM((ND, OWN, WIDE), BF),
            pltpu.VMEM((ND, OWN, WIDE), BF),
            pltpu.VMEM((NC - ND, 4, 64, DW), BF),
            pltpu.VMEM((NC - ND, 4, 64, DW), BF),
            pltpu.VMEM((OWN, D), F32),
            dma((NW, 2)),
            dma((7,)),
            dma((2, NC, MSG)),
            dma((2, NC, MSG)),
            dma((2, NC, MSG)),
            dma((2, NC, MSG)),
            dma((3,)),
            dma((3,)),
        ],
        compiler_params=pltpu.CompilerParams(
            collective_id=0, has_side_effects=True, vmem_limit_bytes=VMEM_GRANT
        ),
        cost_estimate=pl.CostEstimate(
            flops=16 * 10**9, bytes_accessed=18 * 10**6, transcendentals=TOK * HID
        ),
        name="gather_compute_scatter",
    )(*arrays, fragment_rows.reshape(1, FRAG))


def copy_kernel(*refs):
    n = len(STATE)
    sems = refs[-1]
    copies = [
        pltpu.make_async_copy(refs[k], refs[n + k].at[0] if k == 0 else refs[n + k], sems.at[k])
        for k in range(n)
    ]
    for copy in copies:
        copy.start()
    for copy in copies:
        copy.wait()


def copy_out(results):
    n = len(STATE)
    return pl.pallas_call(
        copy_kernel,
        out_shape=STATE,
        in_specs=[pl.BlockSpec(memory_space=pltpu.VMEM)] * n,
        out_specs=(pl.BlockSpec(memory_space=pl.ANY),) * n,
        scratch_shapes=[pltpu.SemaphoreType.DMA((n,))],
        compiler_params=pltpu.CompilerParams(vmem_limit_bytes=8 * 2**20),
        name="copy_out",
    )(*results)


def per_device(
    tokens, w_gate, w_up, d_hidden, outer_rows, outer_momentum, adam_first, adam_second, fragment_rows
):
    return copy_out(
        exchange(
            tokens, w_gate, w_up, d_hidden, outer_rows, outer_momentum, adam_first, adam_second,
            fragment_rows,
        )
    )


def solution(mesh):
    return jax.shard_map(
        per_device,
        mesh=mesh,
        in_specs=(
            P("island", "fsdp", None),
            P("island", None, "fsdp"),
            P("island", None, "fsdp"),
            P("island", None, "fsdp"),
            P(None, None, "fsdp"),
            P(None, None, "fsdp"),
            P("island", None, None, "fsdp"),
            P("island", None, None, "fsdp"),
            P(),
        ),
        out_specs=(
            P("island", "fsdp", None),
            P("island", None, None, "fsdp"),
            P(None, None, "fsdp"),
            P(None, None, "fsdp"),
            P("island", None, None, "fsdp"),
            P("island", None, None, "fsdp"),
        ),
        check_vma=False,
    )
```
